32 devices in a mesh: groups: 1, expert: 8 (over z, y), dp: 2 (over x), seq: 2 (over core).
Axes of the slice: x: 2, y: 2, z: 4, core: 2. Of those that a mesh axis runs over, the one named last changes fastest.
Arguments:
- hidden_rows: bfloat16 [4096, 1024], P(('groups', 'expert', 'dp', 'seq')), may hold values from -6 to 6
- out_grad: bfloat16 [4096, 1024], P(('groups', 'expert', 'dp', 'seq')), may hold values from -3 to 3
- gates: float32 [4096, 6], P(('groups', 'expert', 'dp', 'seq')), may hold values from 0.1 to 0.6
- routes: int32 [4096, 6], P(('groups', 'expert', 'dp', 'seq')), may hold values from 0 to 15, all different within a row; in each aligned block of 128 rows (0 to 127, 128 to 255, ...) at most 49 rows name the same one
- w_gate: bfloat16 [16, 1024, 704], P(('expert', 'seq'), None, 'dp'), may hold values from -0.1875 to 0.1875
- w_up: bfloat16 [16, 1024, 704], P(('expert', 'seq'), None, 'dp'), may hold values from -0.1875 to 0.1875
- w_down: bfloat16 [16, 704, 1024], P(('expert', 'seq'), 'dp'), may hold values from -0.21875 to 0.21875
Outputs:
- mixed: bfloat16 [4096, 1024], P(('groups', 'expert', 'dp', 'seq'))
- grad_rows: bfloat16 [4096, 1024], P(('groups', 'expert', 'dp', 'seq'))
- grad_gates: float32 [4096, 6], P(('groups', 'expert', 'dp', 'seq'))
The draws below stay inside these ranges and needn't reach their ends.
Inputs may be any that keep to these rules, and one draw needn't show every extreme that they name: `routes`: the 6 entries of a row differ. Among the rows of one device no expert is named more than 49 times, and in every draw some device names some expert exactly 49 times.
All inputs are finite; a program needn't handle non-finite values.
Results may differ from the reference program's by a relative error of at most 0.0065.
Values may be sent and summed in bfloat16 or wider, within the bound.
No kernel may reach another device: no remote copies, remote signals or barrier semaphores. Data moves between devices by JAX's collectives and lax.ppermute only.
A program may use at most 64 MiB of HBM per device.

```python
import math
import jax
import jax.numpy as jnp
import numpy as np
from jax import lax

D = 1024
FFE = 704
TOP = 6
TOK_DEV = 128
EXPERTS = 16
TOKENS = 4096
CAP = 49


def level_of(key, extent, split, low, high):
    factor_of, own = 1.0, jax.random.fold_in(key, 6)
    for dim, shards_of in split:
        steps = jnp.exp(jax.random.uniform(jax.random.fold_in(own, dim), (shards_of,), jnp.float32, low / len(split), high / len(split)))
        factor_of = factor_of * jnp.repeat(steps, extent[dim] // shards_of).reshape([-1 if axis == dim else 1 for axis in range(len(extent))])
    return factor_of


def routed_block(stream_key, own, number, rows, amount, top, limit, lean):
    ranking = jax.random.permutation(stream_key, amount)
    crowded, usual = shares(amount, rows * top, limit, lean, True), shares(amount, rows * top, limit, lean, False)
    places = jnp.arange(amount)

    def named(tallies, rotation):
        used = int((tallies > 0).sum())
        fixed = max(1, used // 4)
        shifted = fixed + (places - fixed + rotation * (used - fixed)) % max(1, amount - fixed)
        return jnp.zeros((amount,), jnp.int32).at[ranking[jnp.where(places < fixed, places, shifted)]].set(jnp.asarray(tallies, jnp.int32))

    tallies = jnp.where(number % 4 == 0, named(crowded, number // 4), named(usual, number - number // 4 - 1))
    mixed = jax.random.permutation(jax.random.fold_in(own, 3), amount)
    giver, sink = mixed[0:amount // 2 * 2:2], mixed[1:amount // 2 * 2:2]
    room = jnp.minimum(tallies[giver] - 1, limit - tallies[sink]) // 2
    room = jnp.where((giver == ranking[0]) | (sink == ranking[0]) | (tallies[sink] == 0), 0, jnp.maximum(room, 0))
    shifted = jax.random.randint(jax.random.fold_in(own, 4), (amount // 2,), 0, 1 << 20) % (room + 1)
    tallies = tallies.at[giver].add(-shifted).at[sink].add(shifted)
    items = jnp.searchsorted(jnp.cumsum(tallies), jnp.arange(rows * top), side="right").astype(jnp.int32)
    listing = items.reshape(top, rows).T
    listing = listing[jax.random.permutation(jax.random.fold_in(own, 1), rows)]
    rotation = jax.random.randint(jax.random.fold_in(own, 2), (rows, 1), 0, top)
    return jnp.take_along_axis(listing, (jnp.arange(top)[None, :] + rotation) % top, axis=1)


def shares(count, total, bound, skew, full):
    weights = [(1 << 20) // math.isqrt(rank ** skew) + 1 for rank in range(1, count + 1)]
    largest = bound if full else min(bound, max(-(-total // count), total * weights[0] // sum(weights)))
    least = 1 if total - largest >= count - 1 else 0
    counts, surplus = [largest] + [least] * (count - 1), total - largest - least * (count - 1)
    while surplus > 0:
        free = [i for i in range(1, count) if counts[i] < largest] or [i for i in range(1, count) if counts[i] < bound]
        whole, budget = sum([weights[i] for i in free]), surplus
        for i in free:
            addition = min(bound - counts[i], max(1, budget * weights[i] // whole), surplus)
            counts[i] = counts[i] + addition
            surplus = surplus - addition
    return np.array(counts)


def normal_values(key, shape, deviation, reach, shards=(), held_as=jnp.bfloat16):
    level = level_of(key, shape, shards, -0.22, 0.18) if shards else 1.0
    drawn = jax.random.normal(key, shape, jnp.float32) * deviation * level
    return jnp.minimum(jnp.maximum(drawn, -reach), reach).astype(held_as)


def setup_inputs(seed: int = 0, part: int = 0) -> dict:
    arg_keys = jax.random.split(jax.random.key(seed), 8)
    part_keys = jax.random.split(jax.random.fold_in(arg_keys[7], part), 8)
    hidden_rows = normal_values(part_keys[0], (TOKENS, D), 1.0, 6.0, ((0, 32),))
    out_grad = normal_values(part_keys[1], (TOKENS, D), 0.5, 3.0, ((0, 32),))
    gates = jnp.clip(0.1 + 0.5 * jax.random.uniform(part_keys[2], (TOKENS, TOP), jnp.float32) ** level_of(part_keys[2], (TOKENS, TOP), ((0, 32),), -0.2, 0.2), 0.1, 0.6)
    routes_keys = jax.random.split(jax.random.fold_in(part_keys[3], 1), TOKENS // TOK_DEV)
    routes_turns = jax.random.permutation(jax.random.fold_in(part_keys[3], 3), TOKENS // TOK_DEV)
    routes = jax.vmap(lambda own, number: routed_block(jax.random.fold_in(part_keys[3], 2), own, number, TOK_DEV, EXPERTS, TOP, CAP, 2))(routes_keys, routes_turns).reshape((TOKENS, TOP))
    w_gate = normal_values(arg_keys[4], (EXPERTS, D, FFE), D ** -0.5, 0.1875, ((0, 16), (2, 2)))
    w_up = normal_values(arg_keys[5], (EXPERTS, D, FFE), D ** -0.5, 0.1875, ((0, 16), (2, 2)))
    w_down = normal_values(arg_keys[6], (EXPERTS, FFE, D), FFE ** -0.5, 0.21875, ((0, 16), (1, 2)))
    return {"hidden_rows": hidden_rows, "out_grad": out_grad, "gates": gates, "routes": routes, "w_gate": w_gate, "w_up": w_up, "w_down": w_down}


def expert_pass(rows, scaled, gate_weight, up_weight, down_weight):
    gate_val = jnp.dot(rows, gate_weight, preferred_element_type=jnp.float32)
    up_val = jnp.dot(rows, up_weight, preferred_element_type=jnp.float32)
    sig = jax.nn.sigmoid(gate_val)
    act = (gate_val * sig * up_val).astype(jnp.bfloat16)
    out = jnp.dot(act, down_weight, preferred_element_type=jnp.float32).astype(jnp.bfloat16)
    d_act = jnp.dot(scaled, down_weight.T, preferred_element_type=jnp.float32)
    d_gate = (d_act * up_val * sig * (1.0 + gate_val * (1.0 - sig))).astype(jnp.bfloat16)
    d_up = (d_act * gate_val * sig).astype(jnp.bfloat16)
    back = jnp.dot(d_gate, gate_weight.T, preferred_element_type=jnp.float32)
    back = back + jnp.dot(d_up, up_weight.T, preferred_element_type=jnp.float32)
    return out, back.astype(jnp.bfloat16)


def reference(hidden_rows, out_grad, gates, routes, w_gate, w_up, w_down):
    flat = routes.reshape(-1).astype(jnp.int32)
    total = flat.shape[0]
    gate_flat = gates.reshape(-1)
    most = (TOKENS // TOK_DEV) * CAP

    def one_expert(carry, expert):
        mixed, grads, gate_grad = carry
        picked = jnp.nonzero(flat == expert, size=most, fill_value=total)[0].astype(jnp.int32)
        live = picked < total
        token = jnp.where(live, picked // TOP, 0).astype(jnp.int32)
        gate_val = jnp.where(live, gate_flat[jnp.minimum(picked, total - 1)], 0.0)
        rows = hidden_rows[token]
        cotangent = out_grad[token].astype(jnp.float32)
        scaled = (gate_val[:, None] * cotangent).astype(jnp.bfloat16)
        out, back = expert_pass(rows, scaled, w_gate[expert], w_up[expert], w_down[expert])
        target = jnp.where(live, token, TOKENS).astype(jnp.int32)
        out32 = out.astype(jnp.float32)
        mixed = mixed.at[target].add(gate_val[:, None] * out32, mode="drop")
        grads = grads.at[target].add(back.astype(jnp.float32), mode="drop")
        products = jnp.sum(cotangent * out32, axis=1)
        gate_grad = gate_grad.at[picked].add(products, mode="drop")
        return (mixed, grads, gate_grad), None

    init = (jnp.zeros((TOKENS, D), jnp.float32), jnp.zeros((TOKENS, D), jnp.float32), jnp.zeros((total,), jnp.float32))
    (mixed, grads, gate_grad), _ = lax.scan(one_expert, init, jnp.arange(EXPERTS, dtype=jnp.int32))
    return mixed.astype(jnp.bfloat16), grads.astype(jnp.bfloat16), gate_grad.reshape(TOKENS, TOP)
```

```python
import functools

import jax
import jax.numpy as jnp
from jax import lax
from jax.experimental import pallas as pl
from jax.experimental.pallas import tpu as pltpu
from jax.sharding import PartitionSpec as P

NT = (((1,), (1,)), ((), ()))
NN = (((1,), (0,)), ((), ()))


def dot(a, b, dims):
    return lax.dot_general(a, b, dims, preferred_element_type=jnp.float32)


def expert_kernel(held, parts, x_ref, o_ref, g_ref, *refs):
    pieces, (mixed_ref, back_ref, gate_grad_ref, w_buf, sem) = refs[: 3 * held * parts], refs[3 * held * parts :]
    piece = w_buf.shape[2] // parts

    def copies(e):
        for h in range(parts):
            for kind in range(3):
                src = pieces[(e * parts + h) * 3 + kind]
                yield pltpu.make_async_copy(src, w_buf.at[kind, e, pl.ds(h * piece, piece)], sem.at[e, h, kind])

    for e in range(held):
        for copy in copies(e):
            copy.start()
    x, o = x_ref[...], o_ref[...]
    columns = lax.broadcasted_iota(jnp.int32, gate_grad_ref.shape, 1)
    gate_grads = jnp.zeros(gate_grad_ref.shape, jnp.float32)
    for e in range(held):
        for copy in copies(e):
            copy.wait()
        gate = g_ref[:, e : e + 1]
        gate_val = dot(x, w_buf[0, e], NT)
        up_val = dot(x, w_buf[1, e], NT)
        d_out = dot(o, w_buf[2, e], NT)
        sig = jax.nn.sigmoid(gate_val)
        silu = gate_val * sig
        act = silu * up_val
        gate_grads = jnp.where(columns == e, jnp.sum(act * d_out, axis=1, keepdims=True), gate_grads)
        d_act = gate * d_out
        d_gate = (d_act * up_val * (sig + silu * (1.0 - sig))).astype(jnp.bfloat16)
        d_up = (d_act * silu).astype(jnp.bfloat16)
        mixed = dot((gate * act).astype(jnp.bfloat16), w_buf[2, e], NN)
        back = dot(d_gate, w_buf[0, e], NN) + dot(d_up, w_buf[1, e], NN)
        if e == 0:
            mixed_ref[...] = mixed
            back_ref[...] = back
        else:
            mixed_ref[...] += mixed
            back_ref[...] += back
    gate_grad_ref[...] = gate_grads


def experts_of(x, o, gate, pieces):
    rows, width = x.shape
    held, parts = len(pieces), len(pieces[0])
    hidden = parts * pieces[0][0][0].shape[0]
    flat = [w for of_expert in pieces for part in of_expert for w in part]
    vmem = pl.BlockSpec(memory_space=pltpu.VMEM)
    return pl.pallas_call(
        functools.partial(expert_kernel, held, parts),
        out_shape=(
            jax.ShapeDtypeStruct((rows, width), jnp.float32),
            jax.ShapeDtypeStruct((rows, width), jnp.float32),
            jax.ShapeDtypeStruct((rows, 128), jnp.float32),
        ),
        in_specs=[vmem] * 3 + [pl.BlockSpec(memory_space=pl.ANY)] * len(flat),
        out_specs=(vmem,) * 3,
        scratch_shapes=[
            pltpu.VMEM((3, held, hidden, width), jnp.bfloat16),
            pltpu.SemaphoreType.DMA((held, parts, 3)),
        ],
        compiler_params=pltpu.CompilerParams(vmem_limit_bytes=40 << 20),
        cost_estimate=pl.CostEstimate(
            flops=12 * rows * width * hidden * held,
            bytes_accessed=6 * hidden * width * held + 12 * rows * width,
            transcendentals=rows * hidden * held,
        ),
    )(x, o, gate, *flat)


def ring_order(n):
    return [0, 2, 4, 6, 7, 5, 3, 1] if n == 8 else list(range(n))


def local(hidden_rows, out_grad, gates, routes, w_gate, w_up, w_down):
    tokens, width = hidden_rows.shape
    n, n_dp, n_seq = lax.axis_size("expert"), lax.axis_size("dp"), lax.axis_size("seq")
    here = w_gate.shape[0]
    experts = n * n_seq * here
    order = ring_order(n)
    fw = [(order[i], order[(i + 1) % n]) for i in range(n)]
    bw = [(b, a) for a, b in fw]
    place = jnp.array([order.index(i) for i in range(n)], jnp.int32)
    at_place = jnp.array(order, jnp.int32)
    me = lax.axis_index("expert")
    my_seq = lax.axis_index("seq")
    my_place = place[me]

    def shifted(a, axis, size, by):
        return lax.ppermute(a, axis, [((i + by) % size, i) for i in range(size)])

    names = jnp.arange(experts, dtype=jnp.int32)
    chosen = routes[:, :, None] == names
    dense = jnp.sum(jnp.where(chosen, gates[:, :, None], 0.0), axis=1)
    dense_all = lax.all_gather(dense, "expert", axis=0)
    wanted = jnp.concatenate(
        [(me * n_seq + (my_seq + r) % n_seq) * here + jnp.arange(here, dtype=jnp.int32) for r in range(n_seq)]
    )
    gate_of = jnp.einsum("jte,he->jth", dense_all, (wanted[:, None] == names).astype(jnp.float32), precision="highest")

    def gates_at(distance):
        return lax.dynamic_index_in_dim(gate_of, at_place[(my_place + distance) % n], 0, keepdims=False)

    kinds = [w_down] + [jnp.swapaxes(w, 1, 2) for w in (w_gate, w_up)]
    by_dp = [kinds] + [[shifted(w, "dp", n_dp, r) for w in kinds] for r in range(1, n_dp)]
    by_seq = [by_dp] + [[[shifted(w, "seq", n_seq, r) for w in share] for share in by_dp] for r in range(1, n_seq)]
    pieces = [
        [(share[1][l], share[2][l], share[0][l]) for share in of_core] for of_core in by_seq for l in range(here)
    ]

    own = jnp.stack([hidden_rows, out_grad])
    ahead, behind = (n - 1) // 2, (n - 1) // 2
    half = tokens // 2
    arrived = {0: own}
    for s in range(1, ahead + 1):
        arrived[-s] = lax.ppermute(arrived[1 - s], "expert", fw)
        arrived[s] = lax.ppermute(arrived[s - 1], "expert", bw)
    far = n // 2
    even = n % 2 == 0
    if even:
        top = lax.ppermute(arrived[1 - far][:, :half], "expert", fw)
        low = lax.ppermute(arrived[far - 1][:, half:], "expert", bw)
        arrived[far] = jnp.concatenate([top, low], axis=1)

    gate_grads = {}

    def block(distances):
        both = [arrived[d] for d in distances]
        x = jnp.concatenate([b[0] for b in both]) if len(both) > 1 else both[0][0]
        o = jnp.concatenate([b[1] for b in both]) if len(both) > 1 else both[0][1]
        gate = jnp.concatenate([gates_at(d) for d in distances])
        mixed, back, grads = experts_of(x, o, gate, pieces)
        for i, d in enumerate(distances):
            gate_grads[d % n] = grads[i * tokens : (i + 1) * tokens, : n_seq * here]
        return [(mixed[i * tokens : (i + 1) * tokens], back[i * tokens : (i + 1) * tokens]) for i in range(len(distances))]

    def rounded(a):
        return a.astype(jnp.bfloat16)

    def plus(part, travelled):
        return part + travelled.astype(jnp.float32)

    send_fw = send_bw = None
    if even:
        ((mixed, back),) = block([far])
        send_fw = [lax.ppermute(rounded(a[:half]), "expert", fw) for a in (mixed, back)]
        send_bw = [lax.ppermute(rounded(a[half:]), "expert", bw) for a in (mixed, back)]
    for s in range(ahead, 0, -1):
        if s == 1:
            parts_fw, parts_bw, parts_own = block([1, -1, 0])
        else:
            parts_fw, parts_bw = block([s, -s])
        if send_fw is None:
            out_fw, out_bw = [rounded(a) for a in parts_fw], [rounded(a) for a in parts_bw]
        elif send_fw[0].shape[0] < tokens:
            out_fw = [rounded(jnp.concatenate([plus(a[:half], t), a[half:]])) for a, t in zip(parts_fw, send_fw)]
            out_bw = [rounded(jnp.concatenate([a[:half], plus(a[half:], t)])) for a, t in zip(parts_bw, send_bw)]
        else:
            out_fw = [rounded(plus(a, t)) for a, t in zip(parts_fw, send_fw)]
            out_bw = [rounded(plus(a, t)) for a, t in zip(parts_bw, send_bw)]
        send_fw = [lax.ppermute(a, "expert", fw) for a in out_fw]
        send_bw = [lax.ppermute(a, "expert", bw) for a in out_bw]
    mixed, grad_rows = [
        rounded(plus(plus(a, f), b)) for a, f, b in zip(parts_own, send_fw, send_bw)
    ]

    stacked = jnp.stack([gate_grads[d] for d in range(n)])
    to_device = jnp.take(stacked, (place - my_place) % n, axis=0)
    came = lax.all_to_all(to_device, "expert", split_axis=0, concat_axis=0, tiled=True)
    sender = jnp.arange(experts, dtype=jnp.int32)
    core, slot_here = (sender // here) % n_seq, sender % here
    slot = ((core - my_seq) % n_seq) * here + slot_here
    by_expert = jnp.stack([came[j] for j in range(n)], axis=1).reshape(tokens, experts)
    column = (sender // (n_seq * here)) * (n_seq * here) + slot
    flat = jnp.einsum("te,fe->tf", by_expert, (column[:, None] == sender).astype(jnp.float32), precision="highest")
    grad_gates = jnp.sum(jnp.where(chosen, flat[:, None, :], 0.0), axis=2)
    return (mixed, grad_rows, grad_gates)


def solution(mesh):
    tokens = P(("groups", "expert", "dp", "seq"), None)
    in_specs = (tokens,) * 4 + (P(("expert", "seq"), None, "dp"),) * 2 + (P(("expert", "seq"), "dp", None),)
    return jax.shard_map(local, mesh=mesh, in_specs=in_specs, out_specs=(tokens,) * 3, check_vma=False)
```

```python
import functools

import jax
import jax.numpy as jnp
from jax import lax
from jax.experimental import pallas as pl
from jax.experimental.pallas import tpu as pltpu
from jax.sharding import PartitionSpec as P

NT = (((1,), (1,)), ((), ()))
NN = (((1,), (0,)), ((), ()))


def dot(a, b, dims):
    return lax.dot_general(a, b, dims, preferred_element_type=jnp.float32)


def part_kernel(layout, blocks, has_prior, is_last, *refs):
    held = len(layout)
    arrays = sum(len(of_expert) for of_expert in layout)
    block_refs, gate_ref, refs = refs[:blocks], refs[blocks], refs[blocks + 1 :]
    weight_refs, refs = refs[:arrays], refs[arrays:]
    prior, refs = (refs[:3], refs[3:]) if has_prior else ((), refs)
    results, (token_buf, weight_buf, mixed_buf, back_buf, grad_buf, token_sem, weight_sem, sum_sem) = refs[:3], refs[3:]
    tokens = block_refs[0].shape[1]
    rows, hidden = token_buf.shape[1], weight_buf.shape[1]
    share = hidden // held

    def weight_copies(kind):
        copies, index = [], 0
        for e, of_expert in enumerate(layout):
            at = e * share
            for units in of_expert:
                source = weight_refs[index].at[pl.ds(kind * units, units)]
                target = weight_buf.at[kind, pl.ds(at, units)]
                copies.append(pltpu.make_async_copy(source, target, weight_sem.at[kind, index]))
                at, index = at + units, index + 1
        return copies

    def token_copies(which):
        return [
            pltpu.make_async_copy(
                block_refs[b].at[which], token_buf.at[which, pl.ds(b * tokens, tokens)], token_sem.at[which, b]
            )
            for b in range(blocks)
        ]

    sums = (mixed_buf, back_buf, grad_buf)
    prior_copies = [pltpu.make_async_copy(prior[i], sums[i], sum_sem.at[i]) for i in range(len(prior))]

    def start(copies):
        for copy in copies:
            copy.start()

    def wait(copies):
        for copy in copies:
            copy.wait()

    def hand_on(i, value):
        if has_prior:
            wait(prior_copies[i : i + 1])
            value = value + sums[i][...]
        if is_last:
            results[i][...] = value
            return []
        sums[i][...] = value
        copy = pltpu.make_async_copy(sums[i], results[i], sum_sem.at[i])
        copy.start()
        return [copy]

    start(token_copies(0) + weight_copies(0) + weight_copies(1) + token_copies(1) + weight_copies(2) + prior_copies)
    unit = lax.broadcasted_iota(jnp.int32, (rows, hidden), 1)
    gate = jnp.broadcast_to(gate_ref[:, 0:1], (rows, hidden))
    for e in range(1, held):
        gate = jnp.where(unit >= e * share, gate_ref[:, e : e + 1], gate)
    wait(token_copies(0) + weight_copies(0))
    gate_val = dot(token_buf[0], weight_buf[0], NT)
    wait(weight_copies(1))
    up_val = dot(token_buf[0], weight_buf[1], NT)
    wait(token_copies(1) + weight_copies(2))
    d_out = dot(token_buf[1], weight_buf[2], NT)
    sig = jax.nn.sigmoid(gate_val)
    silu = gate_val * sig
    act = silu * up_val
    d_act = gate * d_out
    d_gate = (d_act * up_val * (sig + silu * (1.0 - sig))).astype(jnp.bfloat16)
    d_up = (d_act * silu).astype(jnp.bfloat16)
    mixed = dot((gate * act).astype(jnp.bfloat16), weight_buf[2], NN)
    leaving = hand_on(0, mixed)
    product = act * d_out
    column = lax.broadcasted_iota(jnp.int32, grad_buf.shape, 1)
    gate_grads = jnp.zeros(grad_buf.shape, jnp.float32)
    for e in range(held):
        mine = (unit >= e * share) & (unit < (e + 1) * share)
        total = jnp.sum(jnp.where(mine, product, 0.0), axis=1, keepdims=True)
        gate_grads = jnp.where(column == e, total, gate_grads)
    leaving += hand_on(2, gate_grads)
    back = dot(d_gate, weight_buf[0], NN) + dot(d_up, weight_buf[1], NN)
    leaving += hand_on(1, back)
    wait(leaving)


def experts_part(blocks, gate, part, prior, is_last):
    tokens, width = blocks[0].shape[1:]
    rows, held = len(blocks) * tokens, len(part)
    layout = [[w.shape[0] // 3 for w in of_expert] for of_expert in part]
    hidden = held * sum(layout[0])
    flat = [w for of_expert in part for w in of_expert]
    vmem, hbm = pl.BlockSpec(memory_space=pltpu.VMEM), pl.BlockSpec(memory_space=pltpu.HBM)
    sums = [(rows, width), (rows, width), (rows, 128)]
    return pl.pallas_call(
        functools.partial(part_kernel, layout, len(blocks), bool(prior), is_last),
        out_shape=tuple(jax.ShapeDtypeStruct(shape, jnp.float32) for shape in sums),
        in_specs=[hbm] * len(blocks) + [vmem] + [hbm] * (len(flat) + len(prior)),
        out_specs=(vmem if is_last else hbm,) * 3,
        scratch_shapes=[
            pltpu.VMEM((2, rows, width), jnp.bfloat16),
            pltpu.VMEM((3, hidden, width), jnp.bfloat16),
            *(pltpu.VMEM(shape, jnp.float32) for shape in sums),
            pltpu.SemaphoreType.DMA((2, len(blocks))),
            pltpu.SemaphoreType.DMA((3, len(flat))),
            pltpu.SemaphoreType.DMA((3,)),
        ],
        compiler_params=pltpu.CompilerParams(vmem_limit_bytes=32 << 20),
        cost_estimate=pl.CostEstimate(
            flops=12 * rows * width * hidden,
            bytes_accessed=6 * hidden * width + 12 * rows * width,
            transcendentals=rows * hidden,
        ),
    )(*blocks, gate, *flat, *prior)


def ring_order(n):
    return [0, 2, 4, 6, 7, 5, 3, 1] if n == 8 else list(range(n))


def after(a, *others):
    return lax.optimization_barrier((a, *others))[0]


def local(hidden_rows, out_grad, gates, routes, w_gate, w_up, w_down):
    tokens, width = hidden_rows.shape
    n, n_dp, n_seq = lax.axis_size("expert"), lax.axis_size("dp"), lax.axis_size("seq")
    here = w_gate.shape[0]
    held = n_seq * here
    experts = n * held
    order = ring_order(n)
    fw = [(order[i], order[(i + 1) % n]) for i in range(n)]
    bw = [(b, a) for a, b in fw]
    me, my_seq = lax.axis_index("expert"), lax.axis_index("seq")
    few = n <= 8
    reach, far, even, half = (n - 1) // 2, n // 2, n % 2 == 0, tokens // 2

    def shifted(a, axis, size, by):
        return lax.ppermute(a, axis, [((i + by) % size, i) for i in range(size)])

    def around(a, way):
        return lax.ppermute(a, "expert", way)

    names = jnp.arange(experts, dtype=jnp.int32)
    chosen = routes.T[None] == names[:, None, None]
    dense = jnp.sum(jnp.where(chosen, gates.T[None], 0.0), axis=1)
    gates_by_chip = lax.all_to_all(dense.reshape(n, held, tokens), "expert", split_axis=0, concat_axis=0, tiled=True)

    units = w_down.shape[1]
    cuts = [0, units // 256 * 256, units] if few and units > 256 and units % 256 else [0, units]
    kinds = [jnp.swapaxes(w_gate, 1, 2), jnp.swapaxes(w_up, 1, 2), w_down]
    own = [
        [jnp.concatenate([w[i, low:high] for w in kinds]) for low, high in zip(cuts, cuts[1:])] for i in range(here)
    ]

    def by_core(share):
        return share + [[shifted(w, "seq", n_seq, r) for w in e] for r in range(1, n_seq) for e in share]

    first = by_core(own)
    groups = [[0, 1, -1]] + [[s, -s] for s in range(2, reach + 1)] + ([[far]] if even else [])

    found = [d % n for group in groups for d in group]
    chips = [[order[(order.index(i) + d) % n] for d in found] for i in range(n)]
    mine = me == jnp.arange(n, dtype=jnp.int32)
    chip_at = jnp.sum(jnp.where(mine[:, None], jnp.array(chips, jnp.int32), 0), axis=0)
    at_chip = chip_at[:, None] == jnp.arange(n, dtype=jnp.int32)
    slots = [[((c + e // here) % n_seq) * here + e % here for e in range(held)] for c in range(n_seq)]
    slot_of = jnp.sum(
        jnp.where((my_seq == jnp.arange(n_seq, dtype=jnp.int32))[:, None], jnp.array(slots, jnp.int32), 0), axis=0
    )
    in_slot = slot_of[:, None] == jnp.arange(held, dtype=jnp.int32)
    picked = at_chip[:, None, :, None] & in_slot[None, :, None, :]
    gate_rows = jnp.sum(jnp.where(picked[..., None], gates_by_chip[None, None], 0.0), axis=(2, 3))
    gate_rows = gate_rows.transpose(0, 2, 1).reshape(n * tokens, held)
    starts = [sum(len(group) for group in groups[:g]) * tokens for g in range(len(groups) + 1)]
    gate_in = [gate_rows[a:b] for a, b in zip(starts, starts[1:])]
    done = [() for _ in groups]
    last = []

    def work(g, part, is_last, *wait_for):
        gate = after(gate_in[g], *last, *wait_for)
        done[g] = experts_part([arrived[d] for d in groups[g]], gate, part, done[g], is_last)
        last[:] = [done[g][2]]

    arrived = {0: jnp.stack([hidden_rows, out_grad])}
    for s in range(1, reach + 1):
        ahead, behind = arrived[1 - s], arrived[s - 1]
        if few and s > 2:
            work(s - 3, first, False)
            ahead, behind = after(ahead, *last), after(behind, *last)
        arrived[-s], arrived[s] = around(ahead, fw), around(behind, bw)
    if few and reach > 1:
        work(reach - 2, first, False)
    if even:
        top = around(after(arrived[1 - far][:, :half], *last), fw)
        low = around(after(arrived[far - 1][:, half:], *last), bw)
        arrived[far] = jnp.concatenate([top, low], axis=1)

    others = []
    for r in range(1, n_dp):
        share = []
        for e in own:
            sent = [w if c == 0 else after(w, arrived[1][0, :1]) for c, w in enumerate(e)]
            share.append([after(shifted(w, "dp", n_dp, r), *last) for w in sent])
        others.append(by_core(share))
    rest = [[w for share in others for w in share[e]] for e in range(held)]
    whole = [first[e] + rest[e] for e in range(held)]
    if few:
        work(reach - 1, first, False)

    def finish(g, *wait_for):
        work(g, rest if done[g] else whole, True, *wait_for)
        mixed, back, _ = done[g]
        return [(mixed[i * tokens : (i + 1) * tokens], back[i * tokens : (i + 1) * tokens]) for i in range(len(groups[g]))]

    def rounded(a):
        return a.astype(jnp.bfloat16)

    def plus(part, travelled):
        return part + travelled.astype(jnp.float32)

    came_fw = came_bw = None
    before = []
    if even:
        ((mixed, back),) = finish(len(groups) - 1)
        came_fw = [around(rounded(a[:half]), fw) for a in (mixed, back)]
        came_bw = [around(rounded(a[half:]), bw) for a in (mixed, back)]
    for s in range(reach, 0, -1):
        sums = finish(s - 1, *before)
        parts_fw, parts_bw = sums[-2:]
        if came_fw is None:
            out_fw, out_bw = [rounded(a) for a in parts_fw], [rounded(a) for a in parts_bw]
        elif came_fw[0].shape[0] < tokens:
            out_fw = [rounded(jnp.concatenate([plus(a[:half], t), a[half:]])) for a, t in zip(parts_fw, came_fw)]
            out_bw = [rounded(jnp.concatenate([a[:half], plus(a[half:], t)])) for a, t in zip(parts_bw, came_bw)]
        else:
            out_fw = [rounded(plus(a, t)) for a, t in zip(parts_fw, came_fw)]
            out_bw = [rounded(plus(a, t)) for a, t in zip(parts_bw, came_bw)]
        before = [] if came_fw is None else [came_fw[0], came_bw[0]]
        came_fw, came_bw = [around(a, fw) for a in out_fw], [around(a, bw) for a in out_bw]
    mixed, grad_rows = [rounded(plus(plus(a, f), b)) for a, f, b in zip(sums[0], came_fw, came_bw)]

    grads = jnp.concatenate([results[2] for results in done])[:, :held].T.reshape(held, n, tokens)
    to_chip = jnp.sum(jnp.where(picked[..., None], grads.transpose(1, 0, 2)[:, :, None, None], 0.0), axis=(0, 1))
    to_chip = after(to_chip, *out_fw, *out_bw)
    by_expert = lax.all_to_all(to_chip, "expert", split_axis=0, concat_axis=0, tiled=True).reshape(experts, tokens)
    grad_gates = jnp.sum(jnp.where(chosen, by_expert[:, None, :], 0.0), axis=0).T
    return (mixed, grad_rows, grad_gates)


def solution(mesh):
    tokens = P(("groups", "expert", "dp", "seq"), None)
    in_specs = (tokens,) * 4 + (P(("expert", "seq"), None, "dp"),) * 2 + (P(("expert", "seq"), "dp", None),)
    return jax.shard_map(local, mesh=mesh, in_specs=in_specs, out_specs=(tokens,) * 3, check_vma=False)
```

```python
import functools

import jax
import jax.numpy as jnp
from jax import lax
from jax.experimental import pallas as pl
from jax.experimental.pallas import tpu as pltpu
from jax.sharding import PartitionSpec as P

NT = (((1,), (1,)), ((), ()))
NN = (((1,), (0,)), ((), ()))


def dot(a, b, dims):
    return lax.dot_general(a, b, dims, preferred_element_type=jnp.float32)


def part_kernel(layout, arrays, blocks, tokens, lines, prior_row, is_last, *refs):
    has_prior = prior_row is not None
    expert_ref, block_refs, refs = refs[0], refs[1 : blocks + 1], refs[blocks + 1 :]
    weight_refs, refs = refs[:arrays], refs[arrays:]
    prior, refs = (refs[:3], refs[3:]) if has_prior else ((), refs)
    results, refs = (refs[:1], refs[1:]) if is_last else (refs[:3], refs[3:])
    token_buf, name_buf, gate_buf, mixed_buf, back_buf, grad_buf, token_sem, sum_sem = refs
    rows, width = mixed_buf.shape
    extra, held = name_buf.shape[1], expert_ref.shape[0]

    per_row = width // tokens
    line = lax.broadcasted_iota(jnp.int32, (extra, width), 0)
    spot = lax.broadcasted_iota(jnp.int32, (extra, width), 1) // tokens

    def token_copies(which):
        return [
            pltpu.make_async_copy(
                block_refs[b].at[pl.ds(which * tokens, tokens)],
                token_buf.at[which, pl.ds(b * tokens, tokens)],
                token_sem.at[which, b],
            )
            for b in range(blocks)
        ]

    name_copies = [
        pltpu.make_async_copy(block_refs[b].at[pl.ds(2 * tokens, extra)], name_buf.at[b], token_sem.at[2, b])
        for b in range(blocks)
    ]

    sums = (mixed_buf, back_buf, grad_buf)
    prior_copies = [pltpu.make_async_copy(prior[i].at[pl.ds(prior_row, rows)], sums[i], sum_sem.at[i]) for i in range(len(prior))]

    def start(copies):
        for copy in copies:
            copy.start()

    def wait(copies):
        for copy in copies:
            copy.wait()

    def spread(i, value):
        for b in range(blocks):
            at, of_block = b * (2 * tokens + extra), value[b * tokens : (b + 1) * tokens]
            if i < 2:
                results[0][at + i * tokens : at + (i + 1) * tokens, :] = of_block
                continue
            by_slot, out = of_block.T, jnp.zeros((extra, width), jnp.float32)
            for e in range(held):
                left, name = jnp.concatenate([by_slot[e : e + 1]] * per_row, axis=1), expert_ref[e]
                for third in range(3):
                    piece = left.astype(jnp.bfloat16).astype(jnp.float32)
                    mine = (spot == name % per_row) & (line == third * lines + name // per_row)
                    out = jnp.where(mine, piece, out)
                    left = left - piece
            results[0][at + 2 * tokens : at + 2 * tokens + extra, :] = out

    def hand_on(i, value):
        if has_prior:
            wait(prior_copies[i : i + 1])
            value = value + sums[i][...]
        if is_last:
            spread(i, value)
            return []
        sums[i][...] = value
        copy = pltpu.make_async_copy(sums[i], results[i], sum_sem.at[i])
        copy.start()
        return [copy]

    start(name_copies + token_copies(0) + token_copies(1) + prior_copies)
    slot = lax.broadcasted_iota(jnp.int32, (8, tokens), 0)
    wait(name_copies)
    for b in range(blocks):
        gates = jnp.zeros((8, tokens), jnp.float32)
        held_gates = name_buf[b].astype(jnp.float32)
        for e in range(held):
            name = expert_ref[e]
            mine = (spot == name % per_row) & (line < 3 * lines) & (line % lines == name // per_row)
            found = jnp.sum(jnp.where(mine, held_gates, 0.0), axis=0, keepdims=True)
            found = sum(found[:, i * tokens : (i + 1) * tokens] for i in range(per_row))
            gates = jnp.where(slot == e, found, gates)
        gate_buf[b * tokens : (b + 1) * tokens, 0:8] = gates.T
    column = lax.broadcasted_iota(jnp.int32, grad_buf.shape, 1)
    gate_grads = jnp.zeros(grad_buf.shape, jnp.float32)
    wait(token_copies(0) + token_copies(1))
    mixed = back = 0.0
    for e, units, places in layout:
        w_gate, w_up, w_down = [weight_refs[index][pl.ds(first, units)] for index, first in places]
        gate = gate_buf[:, e : e + 1]
        gate_val = dot(token_buf[0], w_gate, NT)
        up_val = dot(token_buf[0], w_up, NT)
        d_out = dot(token_buf[1], w_down, NT)
        sig = jax.nn.sigmoid(gate_val)
        silu = gate_val * sig
        act = silu * up_val
        d_act = gate * d_out
        d_gate = (d_act * up_val * (sig + silu * (1.0 - sig))).astype(jnp.bfloat16)
        d_up = (d_act * silu).astype(jnp.bfloat16)
        mixed = mixed + dot((gate * act).astype(jnp.bfloat16), w_down, NN)
        total = jnp.sum(act * d_out, axis=1, keepdims=True)
        gate_grads = gate_grads + jnp.where(column == e, total, 0.0)
        back = back + dot(d_gate, w_gate, NN) + dot(d_up, w_up, NN)
    leaving = hand_on(0, mixed)
    leaving += hand_on(2, gate_grads)
    leaving += hand_on(1, back)
    wait(leaving)


def experts_part(blocks, experts_here, lines, tokens, part, prior, prior_row, is_last):
    width = blocks[0].shape[1]
    rows = len(blocks) * tokens
    flat, layout = [], []
    for e, units, places in part:
        known = []
        for array, first in places:
            if not any(array is a for a in flat):
                flat.append(array)
            known.append(([array is a for a in flat].index(True), first))
        layout.append((e, units, known))
    hidden = sum(units for _, units, _ in part)
    vmem, hbm = pl.BlockSpec(memory_space=pltpu.VMEM), pl.BlockSpec(memory_space=pltpu.HBM)
    sums, out = [(rows, width), (rows, width), (rows, 128)], [(len(blocks) * blocks[0].shape[0], width)]
    return pl.pallas_call(
        functools.partial(part_kernel, layout, len(flat), len(blocks), tokens, lines, prior_row if prior else None, is_last),
        out_shape=tuple(jax.ShapeDtypeStruct(shape, jnp.float32) for shape in (out if is_last else sums)),
        in_specs=[pl.BlockSpec(memory_space=pltpu.SMEM)] + [hbm] * len(blocks) + [vmem] * len(flat) + [hbm] * len(prior),
        out_specs=(vmem,) if is_last else (hbm,) * 3,
        scratch_shapes=[
            pltpu.VMEM((2, rows, width), jnp.bfloat16),
            pltpu.VMEM((len(blocks), blocks[0].shape[0] - 2 * tokens, width), jnp.bfloat16),
            pltpu.VMEM((rows, 128), jnp.float32),
            *(pltpu.VMEM(shape, jnp.float32) for shape in sums),
            pltpu.SemaphoreType.DMA((3, len(blocks))),
            pltpu.SemaphoreType.DMA((3,)),
        ],
        compiler_params=pltpu.CompilerParams(vmem_limit_bytes=24 << 20),
        cost_estimate=pl.CostEstimate(
            flops=120 * rows * width * hidden,
            bytes_accessed=60 * hidden * width + 120 * rows * width,
            transcendentals=rows * hidden,
        ),
    )(experts_here, *blocks, *flat, *prior)


def gate_rows(dense, width):
    pieces, left = [], dense.reshape(-1, width)
    for _ in range(3):
        piece = lax.reduce_precision(left, 8, 7)
        pieces.append(piece)
        left = left - piece
    rows = jnp.concatenate(pieces).astype(jnp.bfloat16)
    return jnp.pad(rows, ((0, -rows.shape[0] % 16), (0, 0)))


def ring_order(n):
    return [0, 2, 4, 6, 7, 5, 3, 1] if n == 8 else list(range(n))


def after(a, *others):
    return lax.optimization_barrier((a, *others))[0]


def local(hidden_rows, out_grad, gates, routes, w_gate, w_up, w_down):
    tokens, width = hidden_rows.shape
    n, n_dp, n_seq = lax.axis_size("expert"), lax.axis_size("dp"), lax.axis_size("seq")
    here = w_gate.shape[0]
    held = n_seq * here
    experts = n * held
    order = ring_order(n)
    fw = [(order[i], order[(i + 1) % n]) for i in range(n)]
    bw = [(b, a) for a, b in fw]
    me, my_seq = lax.axis_index("expert"), lax.axis_index("seq")
    few = n <= 8
    reach, far, even, half = (n - 1) // 2, n // 2, n % 2 == 0, tokens // 2

    def shifted(a, axis, size, by):
        return lax.ppermute(a, axis, [((i + by) % size, i) for i in range(size)])

    def around(a, way):
        return lax.ppermute(a, "expert", way)

    names = jnp.arange(experts, dtype=jnp.int32)
    chosen = routes.T[None] == names[:, None, None]
    dense = jnp.sum(jnp.where(chosen, gates.T[None], 0.0), axis=1)

    units = w_down.shape[1]
    own = [[w[i] for w in (jnp.swapaxes(w_gate, 1, 2), jnp.swapaxes(w_up, 1, 2), w_down)] for i in range(here)]

    def listed(arrays, slot):
        return (slot, units, tuple((w, 0) for w in arrays))

    gate_up = [jnp.concatenate(w[:2]) for w in own]

    def packed(both, down, slot):
        return (slot, units, ((both, 0), (both, units), (down, 0)))

    first = [listed(w, i) for i, w in enumerate(own)]
    groups = [[0, 1, -1]] + [[s, -s] for s in range(2, reach + 1)] + ([[far]] if even else [])

    slots = [[((c + e // here) % n_seq) * here + e % here for e in range(held)] for c in range(n_seq)]
    slot_of = jnp.sum(
        jnp.where((my_seq == jnp.arange(n_seq, dtype=jnp.int32))[:, None], jnp.array(slots, jnp.int32), 0), axis=0
    )
    experts_here = me * held + slot_of
    lines = experts * tokens // width
    done = [() for _ in groups]
    last = []

    def work(g, part, is_last, *wait_for, skip=0, take=None):
        named = after(experts_here, *last, *wait_for)
        some = groups[g][skip:take]
        got = experts_part(
            [arrived[d] for d in some], named, lines, tokens, part, done[g], skip * tokens, is_last
        )
        last[:] = [got[-1] if not is_last else got[0][:1]]
        return got

    def top_half(a):
        return jnp.concatenate([a[:half], a[tokens : tokens + half], a[2 * tokens :]])

    def low_half(a):
        return jnp.concatenate([a[half:tokens], a[tokens + half : 2 * tokens]])

    arrived = {0: jnp.concatenate([hidden_rows, out_grad, gate_rows(dense, width)])}
    arrived[-1], arrived[1] = around(arrived[0], fw), around(arrived[0], bw)
    for r in range(1, n_seq):
        for i in range(here):
            down = after(own[i][2], arrived[1][:1]) if few else own[i][2]
            first.append(packed(shifted(gate_up[i], "seq", n_seq, r), shifted(down, "seq", n_seq, r), r * here + i))
    for s in range(2, reach + 1):
        ahead, behind = arrived[1 - s], arrived[s - 1]
        if few and s > 2:
            done[s - 3] = work(s - 3, first, False)
            ahead, behind = after(ahead, *last), after(behind, *last)
        arrived[-s], arrived[s] = around(ahead, fw), around(behind, bw)
    if few and reach > 1:
        done[reach - 2] = work(reach - 2, first, False)
    end = []
    if even:
        ahead, behind = after(arrived[1 - far], *last), after(arrived[far - 1], *last)
        top, low = around(top_half(ahead), fw), around(low_half(behind), bw)
        end = [top[:1], low[:1]]
        arrived[far] = jnp.concatenate([top[:half], low[:half], top[half:tokens], low[half:], top[tokens:]])

    rest = []
    for r in range(1, n_dp):
        for i in range(here):
            down, both = shifted(own[i][2], "dp", n_dp, r), shifted(gate_up[i], "dp", n_dp, r)
            rest.append(packed(both, down, i))
            down, both = after(down, *last, arrived[reach][:1]), after(both, *last, *end)
            for q in range(1, n_seq):
                rest.append(packed(shifted(both, "seq", n_seq, q), shifted(down, "seq", n_seq, q), q * here + i))

    if few:
        done[reach - 1] = work(reach - 1, first, False)

    def finish(g, *wait_for, skip=0, take=None):
        (sums,) = work(g, rest if done[g] else first + rest, True, *wait_for, skip=skip, take=take)
        size = sums.shape[0] // len(groups[g][skip:take])
        return [sums[i * size : (i + 1) * size] for i in range(len(groups[g][skip:take]))]

    def rounded(a):
        return a.astype(jnp.bfloat16)

    def plus(part, travelled):
        return part + travelled.astype(jnp.float32)

    def plus_top(a, t):
        return jnp.concatenate(
            [
                plus(a[:half], t[:half]),
                a[half:tokens],
                plus(a[tokens : tokens + half], t[half:tokens]),
                a[tokens + half : 2 * tokens],
                plus(a[2 * tokens :], t[tokens:]),
            ]
        )

    def plus_low(a, t):
        return jnp.concatenate(
            [
                a[:half],
                plus(a[half:tokens], t[:half]),
                a[tokens : tokens + half],
                plus(a[tokens + half : 2 * tokens], t[half:]),
                a[2 * tokens :],
            ]
        )

    came = None
    if even:
        (sums,) = finish(len(groups) - 1)
        came = around(rounded(top_half(sums)), fw), around(rounded(low_half(sums)), bw)
    before = []
    for s in range(reach, 0, -1):
        sums_fw, sums_bw = finish(s - 1, *before, skip=int(s == 1))
        if came is None:
            out = rounded(sums_fw), rounded(sums_bw)
        elif even and s == reach:
            out = rounded(plus_top(sums_fw, came[0])), rounded(plus_low(sums_bw, came[1]))
        else:
            out = rounded(plus(sums_fw, came[0])), rounded(plus(sums_bw, came[1]))
        before = [] if came is None else [a[:1] for a in came]
        came = around(out[0], fw), around(out[1], bw)
    (own_sums,) = finish(0, *[a[:1] for a in out], take=1)
    total = plus(plus(own_sums, came[0]), came[1])
    mixed, grad_rows = rounded(total[:tokens]), rounded(total[tokens : 2 * tokens])

    thirds = total[2 * tokens : 2 * tokens + 3 * lines].reshape(3, lines, width)
    by_expert = (thirds[0] + thirds[1] + thirds[2]).reshape(experts, tokens)
    grad_gates = jnp.sum(jnp.where(chosen, by_expert[:, None, :], 0.0), axis=0).T
    return (mixed, grad_rows, grad_gates)


def solution(mesh):
    tokens = P(("groups", "expert", "dp", "seq"), None)
    in_specs = (tokens,) * 4 + (P(("expert", "seq"), None, "dp"),) * 2 + (P(("expert", "seq"), "dp", None),)
    return jax.shard_map(local, mesh=mesh, in_specs=in_specs, out_specs=(tokens,) * 3, check_vma=False)
```

```python
import functools

import jax
import jax.numpy as jnp
from jax import lax
from jax.experimental import pallas as pl
from jax.experimental.pallas import tpu as pltpu
from jax.sharding import PartitionSpec as P

NT = (((1,), (1,)), ((), ()))
NN = (((1,), (0,)), ((), ()))


def dot(a, b, dims):
    return lax.dot_general(a, b, dims, preferred_element_type=jnp.float32)


def part_kernel(layout, arrays, blocks, tokens, lines, prior_row, is_last, *refs):
    has_prior = prior_row is not None
    expert_ref, block_refs, refs = refs[0], refs[1 : blocks + 1], refs[blocks + 1 :]
    weight_refs, refs = refs[:arrays], refs[arrays:]
    prior, refs = (refs[:3], refs[3:]) if has_prior else ((), refs)
    results, refs = (refs[:1], refs[1:]) if is_last else (refs[:3], refs[3:])
    token_buf, name_buf, gate_buf, mixed_buf, back_buf, grad_buf, token_sem, sum_sem = refs
    rows, width = mixed_buf.shape
    extra, held = name_buf.shape[1], expert_ref.shape[0]

    per_row = width // tokens
    line = lax.broadcasted_iota(jnp.int32, (extra, width), 0)
    spot = lax.broadcasted_iota(jnp.int32, (extra, width), 1) // tokens

    def token_copies(which):
        return [
            pltpu.make_async_copy(
                block_refs[b].at[pl.ds(which * tokens, tokens)],
                token_buf.at[which, pl.ds(b * tokens, tokens)],
                token_sem.at[which, b],
            )
            for b in range(blocks)
        ]

    name_copies = [
        pltpu.make_async_copy(block_refs[b].at[pl.ds(2 * tokens, extra)], name_buf.at[b], token_sem.at[2, b])
        for b in range(blocks)
    ]

    sums = (mixed_buf, back_buf, grad_buf)
    prior_copies = [pltpu.make_async_copy(prior[i].at[pl.ds(prior_row, rows)], sums[i], sum_sem.at[i]) for i in range(len(prior))]

    def start(copies):
        for copy in copies:
            copy.start()

    def wait(copies):
        for copy in copies:
            copy.wait()

    def spread(i, value):
        for b in range(blocks):
            at, of_block = b * (2 * tokens + extra), value[b * tokens : (b + 1) * tokens]
            if i < 2:
                results[0][at + i * tokens : at + (i + 1) * tokens, :] = of_block
                continue
            by_slot, out = of_block.T, jnp.zeros((extra, width), jnp.float32)
            for e in range(held):
                left, name = jnp.concatenate([by_slot[e : e + 1]] * per_row, axis=1), expert_ref[e]
                for third in range(3):
                    piece = left.astype(jnp.bfloat16).astype(jnp.float32)
                    mine = (spot == name % per_row) & (line == third * lines + name // per_row)
                    out = jnp.where(mine, piece, out)
                    left = left - piece
            results[0][at + 2 * tokens : at + 2 * tokens + extra, :] = out

    def hand_on(i, value):
        if has_prior:
            wait(prior_copies[i : i + 1])
            value = value + sums[i][...]
        if is_last:
            spread(i, value)
            return []
        sums[i][...] = value
        copy = pltpu.make_async_copy(sums[i], results[i], sum_sem.at[i])
        copy.start()
        return [copy]

    start(name_copies + token_copies(0) + token_copies(1) + prior_copies)
    slot = lax.broadcasted_iota(jnp.int32, (8, tokens), 0)
    wait(name_copies)
    for b in range(blocks):
        gates = jnp.zeros((8, tokens), jnp.float32)
        held_gates = name_buf[b].astype(jnp.float32)
        for e in range(held):
            name = expert_ref[e]
            mine = (spot == name % per_row) & (line < 3 * lines) & (line % lines == name // per_row)
            found = jnp.sum(jnp.where(mine, held_gates, 0.0), axis=0, keepdims=True)
            found = sum(found[:, i * tokens : (i + 1) * tokens] for i in range(per_row))
            gates = jnp.where(slot == e, found, gates)
        gate_buf[b * tokens : (b + 1) * tokens, 0:8] = gates.T
    column = lax.broadcasted_iota(jnp.int32, grad_buf.shape, 1)
    gate_grads = jnp.zeros(grad_buf.shape, jnp.float32)
    wait(token_copies(0) + token_copies(1))
    mixed = back = 0.0
    for e, units, places in layout:
        w_gate, w_up, w_down = [weight_refs[index][pl.ds(first, units)] for index, first in places]
        gate = gate_buf[:, e : e + 1]
        gate_val = dot(token_buf[0], w_gate, NT)
        up_val = dot(token_buf[0], w_up, NT)
        d_out = dot(token_buf[1], w_down, NT)
        sig = jax.nn.sigmoid(gate_val)
        silu = gate_val * sig
        act = silu * up_val
        d_act = gate * d_out
        d_gate = (d_act * up_val * (sig + silu * (1.0 - sig))).astype(jnp.bfloat16)
        d_up = (d_act * silu).astype(jnp.bfloat16)
        mixed = mixed + dot((gate * act).astype(jnp.bfloat16), w_down, NN)
        total = jnp.sum(act * d_out, axis=1, keepdims=True)
        gate_grads = gate_grads + jnp.where(column == e, total, 0.0)
        back = back + dot(d_gate, w_gate, NN) + dot(d_up, w_up, NN)
    leaving = hand_on(0, mixed)
    leaving += hand_on(2, gate_grads)
    leaving += hand_on(1, back)
    wait(leaving)


def experts_part(blocks, experts_here, lines, tokens, part, prior, prior_row, is_last):
    width = blocks[0].shape[1]
    rows = len(blocks) * tokens
    flat, layout = [], []
    for e, units, places in part:
        known = []
        for array, first in places:
            if not any(array is a for a in flat):
                flat.append(array)
            known.append(([array is a for a in flat].index(True), first))
        layout.append((e, units, known))
    hidden = sum(units for _, units, _ in part)
    vmem, hbm = pl.BlockSpec(memory_space=pltpu.VMEM), pl.BlockSpec(memory_space=pltpu.HBM)
    sums, out = [(rows, width), (rows, width), (rows, 128)], [(len(blocks) * blocks[0].shape[0], width)]
    return pl.pallas_call(
        functools.partial(part_kernel, layout, len(flat), len(blocks), tokens, lines, prior_row if prior else None, is_last),
        out_shape=tuple(jax.ShapeDtypeStruct(shape, jnp.float32) for shape in (out if is_last else sums)),
        in_specs=[pl.BlockSpec(memory_space=pltpu.SMEM)] + [hbm] * len(blocks) + [vmem] * len(flat) + [hbm] * len(prior),
        out_specs=(vmem,) if is_last else (hbm,) * 3,
        scratch_shapes=[
            pltpu.VMEM((2, rows, width), jnp.bfloat16),
            pltpu.VMEM((len(blocks), blocks[0].shape[0] - 2 * tokens, width), jnp.bfloat16),
            pltpu.VMEM((rows, 128), jnp.float32),
            *(pltpu.VMEM(shape, jnp.float32) for shape in sums),
            pltpu.SemaphoreType.DMA((3, len(blocks))),
            pltpu.SemaphoreType.DMA((3,)),
        ],
        compiler_params=pltpu.CompilerParams(vmem_limit_bytes=24 << 20),
        cost_estimate=pl.CostEstimate(
            flops=120 * rows * width * hidden,
            bytes_accessed=60 * hidden * width + 120 * rows * width,
            transcendentals=rows * hidden,
        ),
    )(experts_here, *blocks, *flat, *prior)


def gate_rows(dense, width):
    pieces, left = [], dense.reshape(-1, width)
    for _ in range(3):
        piece = lax.reduce_precision(left, 8, 7)
        pieces.append(piece)
        left = left - piece
    rows = jnp.concatenate(pieces).astype(jnp.bfloat16)
    return jnp.pad(rows, ((0, -rows.shape[0] % 16), (0, 0)))


def ring_order(n):
    return [0, 2, 4, 6, 7, 5, 3, 1] if n == 8 else list(range(n))


def after(a, *others):
    return lax.optimization_barrier((a, *others))[0]


def local(hidden_rows, out_grad, gates, routes, w_gate, w_up, w_down):
    tokens, width = hidden_rows.shape
    n, n_dp, n_seq = lax.axis_size("expert"), lax.axis_size("dp"), lax.axis_size("seq")
    here = w_gate.shape[0]
    held = n_seq * here
    experts = n * held
    order = ring_order(n)
    fw = [(order[i], order[(i + 1) % n]) for i in range(n)]
    bw = [(b, a) for a, b in fw]
    me, my_seq = lax.axis_index("expert"), lax.axis_index("seq")
    few = n <= 8
    reach, far, even, half = (n - 1) // 2, n // 2, n % 2 == 0, tokens // 2

    def shifted(a, axis, size, by):
        return lax.ppermute(a, axis, [((i + by) % size, i) for i in range(size)])

    def around(a, way):
        return lax.ppermute(a, "expert", way)

    names = jnp.arange(experts, dtype=jnp.int32)
    chosen = routes.T[None] == names[:, None, None]
    dense = jnp.sum(jnp.where(chosen, gates.T[None], 0.0), axis=1)

    units = w_down.shape[1]
    own = [[w[i] for w in (jnp.swapaxes(w_gate, 1, 2), jnp.swapaxes(w_up, 1, 2), w_down)] for i in range(here)]

    def listed(arrays, slot):
        return (slot, units, tuple((w, 0) for w in arrays))

    first = [listed(w, i) for i, w in enumerate(own)]
    to_dp = [list(w) for w in own]
    for r in range(1, n_seq):
        for i in range(here):
            gate, up = shifted(own[i][0], "seq", n_seq, r), shifted(own[i][1], "seq", n_seq, r)
            gate, up, down, *to_dp[i][:2] = lax.optimization_barrier((gate, up, own[i][2], *to_dp[i][:2]))
            first.append(listed([gate, up, shifted(down, "seq", n_seq, r)], r * here + i))

    groups = [[0, 1, -1]] + [[s, -s] for s in range(2, reach + 1)] + ([[far]] if even else [])

    slots = [[((c + e // here) % n_seq) * here + e % here for e in range(held)] for c in range(n_seq)]
    slot_of = jnp.sum(
        jnp.where((my_seq == jnp.arange(n_seq, dtype=jnp.int32))[:, None], jnp.array(slots, jnp.int32), 0), axis=0
    )
    experts_here = me * held + slot_of
    lines = experts * tokens // width
    done = [() for _ in groups]
    last = []

    def work(g, part, is_last, *wait_for, skip=0, take=None):
        named = after(experts_here, *last, *wait_for)
        some = groups[g][skip:take]
        got = experts_part(
            [arrived[d] for d in some], named, lines, tokens, part, done[g], skip * tokens, is_last
        )
        last[:] = [got[-1] if not is_last else got[0][:1]]
        return got

    def top_half(a):
        return jnp.concatenate([a[:half], a[tokens : tokens + half], a[2 * tokens :]])

    def low_half(a):
        return jnp.concatenate([a[half:tokens], a[tokens + half : 2 * tokens]])

    shares = [
        [shifted(w, "dp", n_dp, r) for w in to_dp[i][::-1]][::-1] for r in range(1, n_dp) for i in range(here)
    ]

    arrived = {0: jnp.concatenate([hidden_rows, out_grad, gate_rows(dense, width)])}
    arrived[-1], arrived[1] = around(arrived[0], fw), around(arrived[0], bw)
    for s in range(2, reach + 1):
        ahead, behind = arrived[1 - s], arrived[s - 1]
        if few and s > 2:
            done[s - 3] = work(s - 3, first, False)
            ahead, behind = after(ahead, *last), after(behind, *last)
        arrived[-s], arrived[s] = around(ahead, fw), around(behind, bw)
    if few and reach > 1:
        done[reach - 2] = work(reach - 2, first, False)
    tied = lax.optimization_barrier((arrived[-reach], arrived[reach], [(w[0], w[2]) for w in shares]))
    arrived[-reach], arrived[reach], early = tied
    late = [w[1] for w in shares]
    if even:
        ahead, behind = after(arrived[1 - far], *last), after(arrived[far - 1], *last)
        top, low = around(top_half(ahead), fw), around(low_half(behind), bw)
        top, low, late = lax.optimization_barrier((top, low, late))
        arrived[far] = jnp.concatenate([top[:half], low[:half], top[half:tokens], low[half:], top[tokens:]])
    rest = []
    for k, ((gate, down), up) in enumerate(zip(early, late)):
        share = [gate, up, down]
        rest.append(listed(share, k % here))
        for q in range(1, n_seq):
            rest.append(listed([shifted(w, "seq", n_seq, q) for w in share], q * here + k % here))
    if few:
        done[reach - 1] = work(reach - 1, first, False)

    def finish(g, *wait_for, skip=0, take=None):
        (sums,) = work(g, rest if done[g] else first + rest, True, *wait_for, skip=skip, take=take)
        size = sums.shape[0] // len(groups[g][skip:take])
        return [sums[i * size : (i + 1) * size] for i in range(len(groups[g][skip:take]))]

    def rounded(a):
        return a.astype(jnp.bfloat16)

    def plus(part, travelled):
        return part + travelled.astype(jnp.float32)

    def plus_top(a, t):
        return jnp.concatenate([plus(a[:half], t[:half]), a[half:tokens], plus(a[tokens:], t[half:])])

    def plus_low(a, t):
        return jnp.concatenate([a[:half], plus(a[half:tokens], t), a[tokens:]])

    def two(a):
        return [a[:tokens], a[tokens:]]

    came = None
    if even:
        (sums,) = finish(len(groups) - 1)
        tops = [rounded(jnp.concatenate([a[:half], a[tokens:]])) for a in two(sums)]
        lows = [rounded(a[half:tokens]) for a in two(sums)]
        came = [(around(a, fw), around(b, bw)) for a, b in zip(tops, lows)]
    before = []
    for s in range(reach, 0, -1):
        sums_fw, sums_bw = finish(s - 1, *before, skip=int(s == 1))
        parts = list(zip(two(sums_fw), two(sums_bw)))
        if came is None:
            out = [(rounded(a), rounded(b)) for a, b in parts]
        elif even and s == reach:
            out = [(rounded(plus_top(a, t)), rounded(plus_low(b, u))) for (a, b), (t, u) in zip(parts, came)]
        else:
            out = [(rounded(plus(a, t)), rounded(plus(b, u))) for (a, b), (t, u) in zip(parts, came)]
        before = [] if came is None else [a[:1] for pair in came for a in pair]
        came = [(around(a, fw), around(b, bw)) for a, b in out]
    (own_sums,) = finish(0, *[a[:1] for pair in out for a in pair], take=1)
    mixed, total = [plus(plus(a, t), u) for a, (t, u) in zip(two(own_sums), came)]
    mixed, grad_rows, total = rounded(mixed), rounded(total[:tokens]), total[tokens:]

    thirds = total[: 3 * lines].reshape(3, lines, width)
    by_expert = (thirds[0] + thirds[1] + thirds[2]).reshape(experts, tokens)
    grad_gates = jnp.sum(jnp.where(chosen, by_expert[:, None, :], 0.0), axis=0).T
    return (mixed, grad_rows, grad_gates)


def solution(mesh):
    tokens = P(("groups", "expert", "dp", "seq"), None)
    in_specs = (tokens,) * 4 + (P(("expert", "seq"), None, "dp"),) * 2 + (P(("expert", "seq"), "dp", None),)
    return jax.shard_map(local, mesh=mesh, in_specs=in_specs, out_specs=(tokens,) * 3, check_vma=False)
```

```python
import functools

import jax
import jax.numpy as jnp
from jax import lax
from jax.experimental import pallas as pl
from jax.experimental.pallas import tpu as pltpu
from jax.sharding import PartitionSpec as P

NT = (((1,), (1,)), ((), ()))
NN = (((1,), (0,)), ((), ()))


def dot(a, b, dims):
    return lax.dot_general(a, b, dims, preferred_element_type=jnp.float32)


def part_kernel(layout, arrays, blocks, tokens, lines, has_prior, is_last, *refs):
    expert_ref, block_refs, refs = refs[0], refs[1 : blocks + 1], refs[blocks + 1 :]
    weight_refs, refs = refs[:arrays], refs[arrays:]
    prior, refs = (refs[:3], refs[3:]) if has_prior else ((), refs)
    results, refs = (refs[:1], refs[1:]) if is_last else (refs[:3], refs[3:])
    token_buf, name_buf, gate_buf, mixed_buf, back_buf, grad_buf, token_sem, sum_sem = refs
    rows, width = mixed_buf.shape
    extra, held = name_buf.shape[1], expert_ref.shape[0]

    per_row = width // tokens
    line = lax.broadcasted_iota(jnp.int32, (extra, width), 0)
    spot = lax.broadcasted_iota(jnp.int32, (extra, width), 1) // tokens

    def token_copies(which):
        return [
            pltpu.make_async_copy(
                block_refs[b].at[pl.ds(which * tokens, tokens)],
                token_buf.at[which, pl.ds(b * tokens, tokens)],
                token_sem.at[which, b],
            )
            for b in range(blocks)
        ]

    name_copies = [
        pltpu.make_async_copy(block_refs[b].at[pl.ds(2 * tokens, extra)], name_buf.at[b], token_sem.at[2, b])
        for b in range(blocks)
    ]

    sums = (mixed_buf, back_buf, grad_buf)
    prior_copies = [pltpu.make_async_copy(prior[i], sums[i], sum_sem.at[i]) for i in range(len(prior))]

    def start(copies):
        for copy in copies:
            copy.start()

    def wait(copies):
        for copy in copies:
            copy.wait()

    def spread(i, value):
        for b in range(blocks):
            at, of_block = b * (2 * tokens + extra), value[b * tokens : (b + 1) * tokens]
            if i < 2:
                results[0][at + i * tokens : at + (i + 1) * tokens, :] = of_block
                continue
            by_slot, out = of_block.T, jnp.zeros((extra, width), jnp.float32)
            for e in range(held):
                left, name = jnp.concatenate([by_slot[e : e + 1]] * per_row, axis=1), expert_ref[e]
                for third in range(3):
                    piece = left.astype(jnp.bfloat16).astype(jnp.float32)
                    mine = (spot == name % per_row) & (line == third * lines + name // per_row)
                    out = jnp.where(mine, piece, out)
                    left = left - piece
            results[0][at + 2 * tokens : at + 2 * tokens + extra, :] = out

    def hand_on(i, value):
        if has_prior:
            wait(prior_copies[i : i + 1])
            value = value + sums[i][...]
        if is_last:
            spread(i, value)
            return []
        sums[i][...] = value
        copy = pltpu.make_async_copy(sums[i], results[i], sum_sem.at[i])
        copy.start()
        return [copy]

    start(name_copies + token_copies(0) + token_copies(1) + prior_copies)
    slot = lax.broadcasted_iota(jnp.int32, (8, tokens), 0)
    wait(name_copies)
    for b in range(blocks):
        gates = jnp.zeros((8, tokens), jnp.float32)
        held_gates = name_buf[b].astype(jnp.float32)
        for e in range(held):
            name = expert_ref[e]
            mine = (spot == name % per_row) & (line < 3 * lines) & (line % lines == name // per_row)
            found = jnp.sum(jnp.where(mine, held_gates, 0.0), axis=0, keepdims=True)
            found = sum(found[:, i * tokens : (i + 1) * tokens] for i in range(per_row))
            gates = jnp.where(slot == e, found, gates)
        gate_buf[b * tokens : (b + 1) * tokens, 0:8] = gates.T
    column = lax.broadcasted_iota(jnp.int32, grad_buf.shape, 1)
    gate_grads = jnp.zeros(grad_buf.shape, jnp.float32)
    wait(token_copies(0) + token_copies(1))
    mixed = back = 0.0
    for e, units, places in layout:
        w_gate, w_up, w_down = [weight_refs[index][pl.ds(first, units)] for index, first in places]
        gate = gate_buf[:, e : e + 1]
        gate_val = dot(token_buf[0], w_gate, NT)
        up_val = dot(token_buf[0], w_up, NT)
        d_out = dot(token_buf[1], w_down, NT)
        sig = jax.nn.sigmoid(gate_val)
        silu = gate_val * sig
        act = silu * up_val
        d_act = gate * d_out
        d_gate = (d_act * up_val * (sig + silu * (1.0 - sig))).astype(jnp.bfloat16)
        d_up = (d_act * silu).astype(jnp.bfloat16)
        mixed = mixed + dot((gate * act).astype(jnp.bfloat16), w_down, NN)
        total = jnp.sum(act * d_out, axis=1, keepdims=True)
        gate_grads = gate_grads + jnp.where(column == e, total, 0.0)
        back = back + dot(d_gate, w_gate, NN) + dot(d_up, w_up, NN)
    leaving = hand_on(0, mixed)
    leaving += hand_on(2, gate_grads)
    leaving += hand_on(1, back)
    wait(leaving)


def experts_part(blocks, experts_here, lines, tokens, part, prior, is_last):
    width = blocks[0].shape[1]
    rows = len(blocks) * tokens
    flat, layout = [], []
    for e, units, places in part:
        known = []
        for array, first in places:
            if not any(array is a for a in flat):
                flat.append(array)
            known.append(([array is a for a in flat].index(True), first))
        layout.append((e, units, known))
    hidden = sum(units for _, units, _ in part)
    vmem, hbm = pl.BlockSpec(memory_space=pltpu.VMEM), pl.BlockSpec(memory_space=pltpu.HBM)
    sums, out = [(rows, width), (rows, width), (rows, 128)], [(len(blocks) * blocks[0].shape[0], width)]
    return pl.pallas_call(
        functools.partial(part_kernel, layout, len(flat), len(blocks), tokens, lines, bool(prior), is_last),
        out_shape=tuple(jax.ShapeDtypeStruct(shape, jnp.float32) for shape in (out if is_last else sums)),
        in_specs=[pl.BlockSpec(memory_space=pltpu.SMEM)] + [hbm] * len(blocks) + [vmem] * len(flat) + [hbm] * len(prior),
        out_specs=(vmem,) if is_last else (hbm,) * 3,
        scratch_shapes=[
            pltpu.VMEM((2, rows, width), jnp.bfloat16),
            pltpu.VMEM((len(blocks), blocks[0].shape[0] - 2 * tokens, width), jnp.bfloat16),
            pltpu.VMEM((rows, 128), jnp.float32),
            *(pltpu.VMEM(shape, jnp.float32) for shape in sums),
            pltpu.SemaphoreType.DMA((3, len(blocks))),
            pltpu.SemaphoreType.DMA((3,)),
        ],
        compiler_params=pltpu.CompilerParams(vmem_limit_bytes=24 << 20),
        cost_estimate=pl.CostEstimate(
            flops=120 * rows * width * hidden,
            bytes_accessed=60 * hidden * width + 120 * rows * width,
            transcendentals=rows * hidden,
        ),
    )(experts_here, *blocks, *flat, *prior)


def gate_rows(dense, width):
    pieces, left = [], dense.reshape(-1, width)
    for _ in range(3):
        piece = lax.reduce_precision(left, 8, 7)
        pieces.append(piece)
        left = left - piece
    rows = jnp.concatenate(pieces).astype(jnp.bfloat16)
    return jnp.pad(rows, ((0, -rows.shape[0] % 16), (0, 0)))


def ring_order(n):
    return [0, 2, 4, 6, 7, 5, 3, 1] if n == 8 else list(range(n))


def after(a, *others):
    return lax.optimization_barrier((a, *others))[0]


def local(hidden_rows, out_grad, gates, routes, w_gate, w_up, w_down):
    tokens, width = hidden_rows.shape
    n, n_dp, n_seq = lax.axis_size("expert"), lax.axis_size("dp"), lax.axis_size("seq")
    here = w_gate.shape[0]
    held = n_seq * here
    experts = n * held
    order = ring_order(n)
    fw = [(order[i], order[(i + 1) % n]) for i in range(n)]
    bw = [(b, a) for a, b in fw]
    me, my_seq = lax.axis_index("expert"), lax.axis_index("seq")
    few = n <= 8
    reach, far, even, half = (n - 1) // 2, n // 2, n % 2 == 0, tokens // 2

    def shifted(a, axis, size, by):
        return lax.ppermute(a, axis, [((i + by) % size, i) for i in range(size)])

    def around(a, way):
        return lax.ppermute(a, "expert", way)

    names = jnp.arange(experts, dtype=jnp.int32)
    chosen = routes.T[None] == names[:, None, None]
    dense = jnp.sum(jnp.where(chosen, gates.T[None], 0.0), axis=1)

    units = w_down.shape[1]
    own = [[w[i] for w in (jnp.swapaxes(w_gate, 1, 2), jnp.swapaxes(w_up, 1, 2), w_down)] for i in range(here)]

    def listed(arrays, slot):
        return (slot, units, tuple((w, 0) for w in arrays))

    first = [listed(w, i) for i, w in enumerate(own)]
    for r in range(1, n_seq):
        for i in range(here):
            first.append(listed([shifted(w, "seq", n_seq, r) for w in own[i]], r * here + i))

    groups = [[0]] + [[s, -s] for s in range(1, reach + 1)] + ([[far]] if even else [])

    slots = [[((c + e // here) % n_seq) * here + e % here for e in range(held)] for c in range(n_seq)]
    slot_of = jnp.sum(
        jnp.where((my_seq == jnp.arange(n_seq, dtype=jnp.int32))[:, None], jnp.array(slots, jnp.int32), 0), axis=0
    )
    experts_here = me * held + slot_of
    lines = experts * tokens // width
    done = [() for _ in groups]
    last = []

    def work(g, part, is_last, *wait_for):
        named = after(experts_here, *last, *wait_for)
        got = experts_part(
            [arrived[d] for d in groups[g]], named, lines, tokens, part, done[g], is_last
        )
        last[:] = [got[-1] if not is_last else got[0][:1]]
        return got

    def top_half(a):
        return jnp.concatenate([a[:half], a[tokens : tokens + half], a[2 * tokens :]])

    def low_half(a):
        return jnp.concatenate([a[half:tokens], a[tokens + half : 2 * tokens]])

    shares = [
        [shifted(w, "dp", n_dp, r) for w in own[i][::-1]][::-1] for r in range(1, n_dp) for i in range(here)
    ]

    arrived = {0: jnp.concatenate([hidden_rows, out_grad, gate_rows(dense, width)])}
    arrived[-1], arrived[1] = around(arrived[0], fw), around(arrived[0], bw)
    for s in range(2, reach + 1):
        ahead, behind = arrived[1 - s], arrived[s - 1]
        if few:
            done[s - 2] = work(s - 2, first, False)
            ahead, behind = after(ahead, *last), after(behind, *last)
        arrived[-s], arrived[s] = around(ahead, fw), around(behind, bw)
    if few and reach > 1:
        done[reach - 1] = work(reach - 1, first, False)
    tied = lax.optimization_barrier((arrived[-reach], arrived[reach], [(w[0], w[2]) for w in shares]))
    arrived[-reach], arrived[reach], early = tied
    late = [w[1] for w in shares]
    if even:
        ahead, behind = after(arrived[1 - far], *last), after(arrived[far - 1], *last)
        top, low = around(top_half(ahead), fw), around(low_half(behind), bw)
        top, low, late = lax.optimization_barrier((top, low, late))
        arrived[far] = jnp.concatenate([top[:half], low[:half], top[half:tokens], low[half:], top[tokens:]])
    rest = []
    for k, ((gate, down), up) in enumerate(zip(early, late)):
        share = [gate, up, down]
        rest.append(listed(share, k % here))
        for q in range(1, n_seq):
            rest.append(listed([shifted(w, "seq", n_seq, q) for w in share], q * here + k % here))
    if few:
        done[reach] = work(reach, first, False)

    def finish(g, *wait_for):
        (sums,) = work(g, rest if done[g] else first + rest, True, *wait_for)
        size = sums.shape[0] // len(groups[g])
        return [sums[i * size : (i + 1) * size] for i in range(len(groups[g]))]

    def rounded(a):
        return a.astype(jnp.bfloat16)

    def plus(part, travelled):
        return part + travelled.astype(jnp.float32)

    def plus_top(a, t):
        return jnp.concatenate([plus(a[:half], t[:half]), a[half:tokens], plus(a[tokens:], t[half:])])

    def plus_low(a, t):
        return jnp.concatenate([a[:half], plus(a[half:tokens], t), a[tokens:]])

    def two(a):
        return [a[:tokens], a[tokens:]]

    came = None
    if even:
        (sums,) = finish(len(groups) - 1)
        high, low = around(rounded(top_half(sums)), fw), around(rounded(low_half(sums)), bw)
        came = [(high[:half], low[:half]), (high[half:], low[half:])]
    before = []
    for s in range(reach, 0, -1):
        sums_fw, sums_bw = finish(s, *before)
        parts = list(zip(two(sums_fw), two(sums_bw)))
        if came is None:
            out = [(rounded(a), rounded(b)) for a, b in parts]
        elif even and s == reach:
            out = [(rounded(plus_top(a, t)), rounded(plus_low(b, u))) for (a, b), (t, u) in zip(parts, came)]
        else:
            out = [(rounded(plus(a, t)), rounded(plus(b, u))) for (a, b), (t, u) in zip(parts, came)]
        before = [] if came is None else [a[:1] for pair in came for a in pair]
        came = [(around(a, fw), around(b, bw)) for a, b in out]
    (own_sums,) = finish(0, *[a[:1] for pair in out for a in pair])
    mixed, total = [plus(plus(a, t), u) for a, (t, u) in zip(two(own_sums), came)]
    mixed, grad_rows, total = rounded(mixed), rounded(total[:tokens]), total[tokens:]

    thirds = total[: 3 * lines].reshape(3, lines, width)
    by_expert = (thirds[0] + thirds[1] + thirds[2]).reshape(experts, tokens)
    grad_gates = jnp.sum(jnp.where(chosen, by_expert[:, None, :], 0.0), axis=0).T
    return (mixed, grad_rows, grad_gates)


def solution(mesh):
    tokens = P(("groups", "expert", "dp", "seq"), None)
    in_specs = (tokens,) * 4 + (P(("expert", "seq"), None, "dp"),) * 2 + (P(("expert", "seq"), "dp", None),)
    return jax.shard_map(local, mesh=mesh, in_specs=in_specs, out_specs=(tokens,) * 3, check_vma=False)
```

```python
import functools

import jax
import jax.numpy as jnp
from jax import lax
from jax.experimental import pallas as pl
from jax.experimental.pallas import tpu as pltpu
from jax.sharding import PartitionSpec as P

NT = (((1,), (1,)), ((), ()))
NN = (((1,), (0,)), ((), ()))


def dot(a, b, dims):
    return lax.dot_general(a, b, dims, preferred_element_type=jnp.float32)


def part_kernel(layout, arrays, blocks, tokens, lines, has_prior, is_last, *refs):
    expert_ref, block_refs, refs = refs[0], refs[1 : blocks + 1], refs[blocks + 1 :]
    weight_refs, refs = refs[:arrays], refs[arrays:]
    prior, refs = (refs[:3], refs[3:]) if has_prior else ((), refs)
    results, refs = (refs[:1], refs[1:]) if is_last else (refs[:3], refs[3:])
    token_buf, name_buf, gate_buf, mixed_buf, back_buf, grad_buf, token_sem, sum_sem = refs
    rows, width = mixed_buf.shape
    extra, held = name_buf.shape[1], expert_ref.shape[0]

    per_row = width // tokens
    line = lax.broadcasted_iota(jnp.int32, (extra, width), 0)
    spot = lax.broadcasted_iota(jnp.int32, (extra, width), 1) // tokens

    def token_copies(which):
        return [
            pltpu.make_async_copy(
                block_refs[b].at[pl.ds(which * tokens, tokens)],
                token_buf.at[which, pl.ds(b * tokens, tokens)],
                token_sem.at[which, b],
            )
            for b in range(blocks)
        ]

    name_copies = [
        pltpu.make_async_copy(block_refs[b].at[pl.ds(2 * tokens, extra)], name_buf.at[b], token_sem.at[2, b])
        for b in range(blocks)
    ]

    sums = (mixed_buf, back_buf, grad_buf)
    prior_copies = [pltpu.make_async_copy(prior[i], sums[i], sum_sem.at[i]) for i in range(len(prior))]

    def start(copies):
        for copy in copies:
            copy.start()

    def wait(copies):
        for copy in copies:
            copy.wait()

    def spread(i, value):
        for b in range(blocks):
            at, of_block = b * (2 * tokens + extra), value[b * tokens : (b + 1) * tokens]
            if i < 2:
                results[0][at + i * tokens : at + (i + 1) * tokens, :] = of_block
                continue
            by_slot, out = of_block.T, jnp.zeros((extra, width), jnp.float32)
            for e in range(held):
                left, name = jnp.concatenate([by_slot[e : e + 1]] * per_row, axis=1), expert_ref[e]
                for third in range(3):
                    piece = left.astype(jnp.bfloat16).astype(jnp.float32)
                    mine = (spot == name % per_row) & (line == third * lines + name // per_row)
                    out = jnp.where(mine, piece, out)
                    left = left - piece
            results[0][at + 2 * tokens : at + 2 * tokens + extra, :] = out

    def hand_on(i, value):
        if has_prior:
            wait(prior_copies[i : i + 1])
            value = value + sums[i][...]
        if is_last:
            spread(i, value)
            return []
        sums[i][...] = value
        copy = pltpu.make_async_copy(sums[i], results[i], sum_sem.at[i])
        copy.start()
        return [copy]

    start(name_copies + token_copies(0) + token_copies(1) + prior_copies)
    slot = lax.broadcasted_iota(jnp.int32, (8, tokens), 0)
    wait(name_copies)
    for b in range(blocks):
        gates = jnp.zeros((8, tokens), jnp.float32)
        held_gates = name_buf[b].astype(jnp.float32)
        for e in range(held):
            name = expert_ref[e]
            mine = (spot == name % per_row) & (line < 3 * lines) & (line % lines == name // per_row)
            found = jnp.sum(jnp.where(mine, held_gates, 0.0), axis=0, keepdims=True)
            found = sum(found[:, i * tokens : (i + 1) * tokens] for i in range(per_row))
            gates = jnp.where(slot == e, found, gates)
        gate_buf[b * tokens : (b + 1) * tokens, 0:8] = gates.T
    column = lax.broadcasted_iota(jnp.int32, grad_buf.shape, 1)
    gate_grads = jnp.zeros(grad_buf.shape, jnp.float32)
    wait(token_copies(0) + token_copies(1))
    mixed = back = 0.0
    for e, units, places in layout:
        w_gate, w_up, w_down = [weight_refs[index][pl.ds(first, units)] for index, first in places]
        gate = gate_buf[:, e : e + 1]
        gate_val = dot(token_buf[0], w_gate, NT)
        up_val = dot(token_buf[0], w_up, NT)
        d_out = dot(token_buf[1], w_down, NT)
        sig = jax.nn.sigmoid(gate_val)
        silu = gate_val * sig
        act = silu * up_val
        d_act = gate * d_out
        d_gate = (d_act * up_val * (sig + silu * (1.0 - sig))).astype(jnp.bfloat16)
        d_up = (d_act * silu).astype(jnp.bfloat16)
        mixed = mixed + dot((gate * act).astype(jnp.bfloat16), w_down, NN)
        total = jnp.sum(act * d_out, axis=1, keepdims=True)
        gate_grads = gate_grads + jnp.where(column == e, total, 0.0)
        back = back + dot(d_gate, w_gate, NN) + dot(d_up, w_up, NN)
    leaving = hand_on(0, mixed)
    leaving += hand_on(2, gate_grads)
    leaving += hand_on(1, back)
    wait(leaving)


def experts_part(blocks, experts_here, lines, tokens, part, prior, is_last):
    width = blocks[0].shape[1]
    rows = len(blocks) * tokens
    flat, layout = [], []
    for e, units, places in part:
        known = []
        for array, first in places:
            if not any(array is a for a in flat):
                flat.append(array)
            known.append(([array is a for a in flat].index(True), first))
        layout.append((e, units, known))
    hidden = sum(units for _, units, _ in part)
    vmem, hbm = pl.BlockSpec(memory_space=pltpu.VMEM), pl.BlockSpec(memory_space=pltpu.HBM)
    sums, out = [(rows, width), (rows, width), (rows, 128)], [(len(blocks) * blocks[0].shape[0], width)]
    return pl.pallas_call(
        functools.partial(part_kernel, layout, len(flat), len(blocks), tokens, lines, bool(prior), is_last),
        out_shape=tuple(jax.ShapeDtypeStruct(shape, jnp.float32) for shape in (out if is_last else sums)),
        in_specs=[pl.BlockSpec(memory_space=pltpu.SMEM)] + [hbm] * len(blocks) + [vmem] * len(flat) + [hbm] * len(prior),
        out_specs=(vmem,) if is_last else (hbm,) * 3,
        scratch_shapes=[
            pltpu.VMEM((2, rows, width), jnp.bfloat16),
            pltpu.VMEM((len(blocks), blocks[0].shape[0] - 2 * tokens, width), jnp.bfloat16),
            pltpu.VMEM((rows, 128), jnp.float32),
            *(pltpu.VMEM(shape, jnp.float32) for shape in sums),
            pltpu.SemaphoreType.DMA((3, len(blocks))),
            pltpu.SemaphoreType.DMA((3,)),
        ],
        compiler_params=pltpu.CompilerParams(vmem_limit_bytes=24 << 20),
        cost_estimate=pl.CostEstimate(
            flops=120 * rows * width * hidden,
            bytes_accessed=60 * hidden * width + 120 * rows * width,
            transcendentals=rows * hidden,
        ),
    )(experts_here, *blocks, *flat, *prior)


def gate_rows(dense, width):
    pieces, left = [], dense.reshape(-1, width)
    for _ in range(3):
        piece = lax.reduce_precision(left, 8, 7)
        pieces.append(piece)
        left = left - piece
    rows = jnp.concatenate(pieces).astype(jnp.bfloat16)
    return jnp.pad(rows, ((0, -rows.shape[0] % 16), (0, 0)))


def ring_order(n):
    return [0, 2, 4, 6, 7, 5, 3, 1] if n == 8 else list(range(n))


def after(a, *others):
    return lax.optimization_barrier((a, *others))[0]


def local(hidden_rows, out_grad, gates, routes, w_gate, w_up, w_down):
    tokens, width = hidden_rows.shape
    n, n_dp, n_seq = lax.axis_size("expert"), lax.axis_size("dp"), lax.axis_size("seq")
    here = w_gate.shape[0]
    held = n_seq * here
    experts = n * held
    order = ring_order(n)
    fw = [(order[i], order[(i + 1) % n]) for i in range(n)]
    bw = [(b, a) for a, b in fw]
    me, my_seq = lax.axis_index("expert"), lax.axis_index("seq")
    few = n <= 8
    reach, far, even, half = (n - 1) // 2, n // 2, n % 2 == 0, tokens // 2

    def shifted(a, axis, size, by):
        return lax.ppermute(a, axis, [((i + by) % size, i) for i in range(size)])

    def around(a, way):
        return lax.ppermute(a, "expert", way)

    names = jnp.arange(experts, dtype=jnp.int32)
    chosen = routes.T[None] == names[:, None, None]
    dense = jnp.sum(jnp.where(chosen, gates.T[None], 0.0), axis=1)

    units = w_down.shape[1]
    own = [[w[i] for w in (jnp.swapaxes(w_gate, 1, 2), jnp.swapaxes(w_up, 1, 2), w_down)] for i in range(here)]

    def listed(arrays, slot):
        return (slot, units, tuple((w, 0) for w in arrays))

    first = [listed(w, i) for i, w in enumerate(own)]
    for r in range(1, n_seq):
        for i in range(here):
            first.append(listed([shifted(w, "seq", n_seq, r) for w in own[i]], r * here + i))

    groups = [[0]] + [[s, -s] for s in range(1, reach + 1)] + ([[far]] if even else [])

    slots = [[((c + e // here) % n_seq) * here + e % here for e in range(held)] for c in range(n_seq)]
    slot_of = jnp.sum(
        jnp.where((my_seq == jnp.arange(n_seq, dtype=jnp.int32))[:, None], jnp.array(slots, jnp.int32), 0), axis=0
    )
    experts_here = me * held + slot_of
    lines = experts * tokens // width
    done = [() for _ in groups]
    last = []

    def work(g, part, is_last, *wait_for):
        named = after(experts_here, *last, *wait_for)
        got = experts_part(
            [arrived[d] for d in groups[g]], named, lines, tokens, part, done[g], is_last
        )
        last[:] = [got[-1] if not is_last else got[0][:1]]
        return got

    def top_half(a):
        return jnp.concatenate([a[:half], a[tokens : tokens + half], a[2 * tokens :]])

    def low_half(a):
        return jnp.concatenate([a[half:tokens], a[tokens + half : 2 * tokens]])

    shares = [
        [shifted(w, "dp", n_dp, r) for w in own[i][::-1]][::-1] for r in range(1, n_dp) for i in range(here)
    ]

    arrived = {0: jnp.concatenate([hidden_rows, out_grad, gate_rows(dense, width)])}
    arrived[-1], arrived[1] = around(arrived[0], fw), around(arrived[0], bw)
    for s in range(2, reach + 1):
        ahead, behind = arrived[1 - s], arrived[s - 1]
        if few:
            done[s - 2] = work(s - 2, first, False)
            ahead, behind = after(ahead, *last), after(behind, *last)
        arrived[-s], arrived[s] = around(ahead, fw), around(behind, bw)
    if few and reach > 1:
        done[reach - 1] = work(reach - 1, first, False)
    arrived[-reach], early = lax.optimization_barrier((arrived[-reach], [(w[0], w[2]) for w in shares]))
    late = [w[1] for w in shares]
    if even:
        ahead, behind = after(arrived[1 - far], *last), after(arrived[far - 1], *last)
        top, low = around(top_half(ahead), fw), around(low_half(behind), bw)
        top, late = lax.optimization_barrier((top, late))
        arrived[far] = jnp.concatenate([top[:half], low[:half], top[half:tokens], low[half:], top[tokens:]])
    rest = []
    for k, ((gate, down), up) in enumerate(zip(early, late)):
        share = [gate, up, down]
        rest.append(listed(share, k % here))
        for q in range(1, n_seq):
            rest.append(listed([shifted(w, "seq", n_seq, q) for w in share], q * here + k % here))
    if few:
        done[reach] = work(reach, first, False)

    def finish(g, *wait_for):
        (sums,) = work(g, rest if done[g] else first + rest, True, *wait_for)
        size = sums.shape[0] // len(groups[g])
        return [sums[i * size : (i + 1) * size] for i in range(len(groups[g]))]

    def rounded(a):
        return a.astype(jnp.bfloat16)

    def plus(part, travelled):
        return part + travelled.astype(jnp.float32)

    def plus_top(a, t):
        return jnp.concatenate([plus(a[:half], t[:half]), a[half:tokens], plus(a[tokens:], t[half:])])

    def plus_low(a, t):
        return jnp.concatenate([a[:half], plus(a[half:tokens], t), a[tokens:]])

    def two(a):
        return [a[:tokens], a[tokens:]]

    came = None
    if even:
        (sums,) = finish(len(groups) - 1)
        high, low = around(rounded(top_half(sums)), fw), around(rounded(low_half(sums)), bw)
        came = [(high[:half], low[:half]), (high[half:], low[half:])]
    before = []
    for s in range(reach, 0, -1):
        sums_fw, sums_bw = finish(s, *before)
        parts = list(zip(two(sums_fw), two(sums_bw)))
        if came is None:
            out = [(rounded(a), rounded(b)) for a, b in parts]
        elif even and s == reach:
            out = [(rounded(plus_top(a, t)), rounded(plus_low(b, u))) for (a, b), (t, u) in zip(parts, came)]
        else:
            out = [(rounded(plus(a, t)), rounded(plus(b, u))) for (a, b), (t, u) in zip(parts, came)]
        before = [] if came is None else [a[:1] for pair in came for a in pair]
        came = [(around(a, fw), around(b, bw)) for a, b in out]
    (own_sums,) = finish(0, *[a[:1] for pair in out for a in pair])
    mixed, total = [plus(plus(a, t), u) for a, (t, u) in zip(two(own_sums), came)]
    mixed, grad_rows, total = rounded(mixed), rounded(total[:tokens]), total[tokens:]

    thirds = total[: 3 * lines].reshape(3, lines, width)
    by_expert = (thirds[0] + thirds[1] + thirds[2]).reshape(experts, tokens)
    grad_gates = jnp.sum(jnp.where(chosen, by_expert[:, None, :], 0.0), axis=0).T
    return (mixed, grad_rows, grad_gates)


def solution(mesh):
    tokens = P(("groups", "expert", "dp", "seq"), None)
    in_specs = (tokens,) * 4 + (P(("expert", "seq"), None, "dp"),) * 2 + (P(("expert", "seq"), "dp", None),)
    return jax.shard_map(local, mesh=mesh, in_specs=in_specs, out_specs=(tokens,) * 3, check_vma=False)
```
